128 devices in a mesh: chan: 32 (over z_hi, y, x), rec: 4 (over z_lo, core).
Axes of the slice: x: 4, y: 4, z: 4 (z_hi: 2, z_lo: 2; z = z_hi * 2 + z_lo), core: 2. Of those that a mesh axis runs over, the one named last changes fastest.
Arguments:
- records: bfloat16 [4, 4096, 8192], P('rec', 'chan'), as said below
- fir_choice: int32 [8192], P('chan'), may hold values from 0 to 15
- bank: float32 [16, 64], replicated, may hold values from -4 to 4
- partner: int32 [3, 32], replicated, may hold values from 0 to 31, as said below
Outputs:
- xcorr: float32 [3, 8192, 8, 256], P(None, 'chan', 'rec')
The draws below stay inside these ranges and needn't reach their ends.
Inputs may be any that keep to these rules, and one draw needn't show every extreme that they name: Each round is a pairing by exclusive or: partner[r, a] = a XOR m_r for one mask m_r of 1 to 31 a round, the masks of different rounds differ. `records`: samples are finite and not all zero in any channel of any record.
All inputs are finite; a program needn't handle non-finite values.
Results may differ from the reference program's by a relative error of at most 0.0055.
Values may be sent and summed in bfloat16 or wider, within the bound.
A program may use at most 128 MiB of HBM per device.

```python
import math
import jax
import jax.numpy as jnp
from jax import lax

BLOCK = 256
TAPS = 64
LAGS = 8
BANKS = 16
ROUNDS = 3
TIME = 4096
NBLK = 32
CHANNELS = 8192
RECORDS = 4


def draw_records(key, part):
    key_scale, key_env, key_base = jax.random.split(key, 3)
    chan_scale = jnp.exp(jax.random.uniform(key_scale, (RECORDS, 1, 1, CHANNELS), jnp.float32, 0.0, math.log(10.0)))
    envelope = jnp.exp(jax.random.uniform(key_env, (RECORDS, TIME // 64, 1, CHANNELS), jnp.float32, math.log(0.3), math.log(3.0)))
    base = jax.random.normal(key_base, (RECORDS, TIME // 64, 64, CHANNELS), jnp.float32)
    values = base * envelope * chan_scale
    return values.reshape(RECORDS, TIME, CHANNELS).astype(jnp.bfloat16)


def draw_partner(key, part):
    masks = (jax.random.permutation(key, NBLK - 1)[:ROUNDS] + 1).astype(jnp.int32)
    blocks = jnp.arange(NBLK, dtype=jnp.int32)
    return jnp.bitwise_xor(blocks[None, :], masks[:, None]).astype(jnp.int32)


def touch_ends(result, own_key, least, top_value):
    index_at = [jax.random.randint(jax.random.fold_in(own_key, axis), (), 0, length) for axis, length in enumerate(result.shape)]
    longest = result.shape.index(max(result.shape))
    beside = index_at[:longest] + [(index_at[longest] + 1) % result.shape[longest]] + index_at[longest + 1:]
    return result.at[tuple(index_at)].set(least).at[tuple(beside)].set(top_value)


def bell_draw(rng, extent, deviation, limit, kind=jnp.bfloat16):
    return jnp.clip(deviation * jax.random.normal(rng, extent, jnp.float32), -limit, limit).astype(kind)


def setup_inputs(seed: int = 0) -> dict:
    splits = jax.random.split(jax.random.key(seed), 5)
    records = draw_records(jax.random.fold_in(splits[4], 71), 0)
    fir_choice = touch_ends(jax.random.randint(splits[1], (CHANNELS,), 0, BANKS), jax.random.fold_in(splits[1], 1), 0, BANKS - 1).astype(jnp.int32)
    bank = bell_draw(splits[2], (BANKS, TAPS), 0.3, 4.0, jnp.float32)
    partner = draw_partner(jax.random.fold_in(splits[4], 71), 0)
    return dict(records=records, fir_choice=fir_choice, bank=bank, partner=partner)


def whiten_one(raw, taps):
    signal = raw.astype(jnp.float32)
    padded = jnp.pad(signal, ((TAPS - 1, 0), (0, 0)))
    total = jnp.zeros(signal.shape, jnp.float32)
    for tap in range(TAPS):
        total = total + taps[:, tap][None, :] * padded[TAPS - 1 - tap:TAPS - 1 - tap + TIME, :]
    whitened = total.astype(jnp.bfloat16)
    values = whitened.astype(jnp.float32)
    power = lax.optimization_barrier(jnp.mean(values * values, axis=0))
    return (values * lax.rsqrt(power + 1e-06)[None, :]).astype(jnp.bfloat16)

def reference(records, fir_choice, bank, partner):
    taps = bank[fir_choice]
    normed = lax.map(lambda raw: whiten_one(raw, taps), records)
    scale = 1.0 / math.sqrt(TIME)
    rounds_out = []
    for step in range(ROUNDS):

        def one_block(block_id):
            start = (block_id * BLOCK).astype(jnp.int32)
            other = (partner[step, block_id] * BLOCK).astype(jnp.int32)
            own = lax.dynamic_slice_in_dim(normed, start, BLOCK, 2)
            mate = lax.dynamic_slice_in_dim(normed, other, BLOCK, 2)
            mate = jnp.pad(mate, ((0, 0), (0, LAGS), (0, 0)))
            total = jnp.zeros((BLOCK, LAGS * BLOCK), jnp.float32)
            for record in range(RECORDS):
                stacked = jnp.concatenate([mate[record, lag:lag + TIME, :] for lag in range(LAGS)], axis=1)
                product = lax.dot_general(own[record], stacked, (((0,), (0,)), ((), ())), preferred_element_type=jnp.float32)
                total = total + product * scale
            return total.reshape(BLOCK, LAGS, BLOCK)
        blocks = lax.map(one_block, jnp.arange(NBLK, dtype=jnp.int32))
        rounds_out.append(blocks.reshape(CHANNELS, LAGS, BLOCK))
    return jnp.stack(rounds_out, axis=0)
```

```python
import functools
import itertools

import jax
import jax.numpy as jnp
from jax import lax
from jax.experimental import pallas as pl
from jax.experimental.pallas import tpu as pltpu
from jax.sharding import PartitionSpec as P

BLOCK = 256
TAPS = 64
LAGS = 8
BANKS = 16
ROUNDS = 3
TIME = 4096
NBLK = 32
SPAN = TIME // NBLK
UNITS = ROUNDS + 1
MESH = pl.DeviceIdType.MESH


def link_loads(move):
    dz, dy, dx = move
    load = [0] * 6
    for first, step in ((0, dx), (2, dy)):
        if step in (1, 2):
            load[first] += 1
        if step in (2, 3):
            load[first + 1] += 1
    if dz:
        load[4] += 1
        load[5] += 1
    return load


def balanced_moves():
    left = [m for m in itertools.product(range(2), range(4), range(4)) if m != (0, 0, 0)]
    total = [0] * 6
    order = []

    def cost(move):
        after = [a + b for a, b in zip(total, link_loads(move))]
        return (max(after) - sum(after) / 6, -sum(link_loads(move)))

    while left:
        best = min(left, key=cost)
        left.remove(best)
        order.append(best)
        total = [a + b for a, b in zip(total, link_loads(best))]
    return order


MOVES = balanced_moves()


def whiten(raw_ref, tt_ref, choice, store):
    def body(w, acc):
        base = pl.multiple_of(w * TAPS, TAPS)
        x = raw_ref[pl.ds(base, 2 * TAPS), :]
        every = jnp.dot(
            tt_ref[...], jnp.concatenate([x, x], axis=0), preferred_element_type=jnp.float32
        )
        out = every[0:TAPS]
        for b in range(1, BANKS):
            out = jnp.where(choice == b, every[b * TAPS : (b + 1) * TAPS], out)
        rounded = out.astype(jnp.bfloat16)
        values = rounded.astype(jnp.float32)
        store(base, rounded, values)
        return acc + (values * values).reshape(TAPS // 8, 8, BLOCK).sum(0)

    acc = lax.fori_loop(0, TIME // TAPS, body, jnp.zeros((8, BLOCK), jnp.float32), unroll=4)
    return lax.rsqrt(acc.sum(0, keepdims=True) * (1.0 / TIME) + 1e-6)


def kernel(
    stage, fir_ref, mate_ref, tt_ref, out_ref,
    raw, choices, ownf, shifted, mate, keep, snd1, rcv1, snd2, rcv2,
    send_sem, recv_sem, local_sem, fir_send, fir_recv, s1_send, s1_recv, s2_send, s2_recv,
):
    me = lax.axis_index("chan")
    rec = lax.axis_index("rec")
    mz, my, mx = me // 16, (me // 4) % 4, me % 4
    core, zlo = rec % 2, rec // 2
    twin = zlo * 2 + (1 - core)
    across = (1 - zlo) * 2 + core

    def peer(move):
        dz, dy, dx = move
        return ((mz + dz) % 2) * 16 + ((my + dy) % 4) * 4 + (mx + dx) % 4

    barrier = pltpu.get_barrier_semaphore()
    for move in MOVES:
        pl.semaphore_signal(barrier, inc=1, device_id=(peer(move), rec), device_id_type=MESH)
    pl.semaphore_signal(barrier, inc=1, device_id=(me, twin), device_id_type=MESH)
    pl.semaphore_signal(barrier, inc=1, device_id=(me, across), device_id_type=MESH)
    pl.semaphore_wait(barrier, len(MOVES) + 2)

    mine = pl.ds(pl.multiple_of(TAPS + me * SPAN, TAPS), SPAN)

    def local_copy(unit):
        return pltpu.make_async_copy(stage.at[unit, me], raw.at[unit, mine], local_sem.at[unit])

    def send_unit(unit, carry):
        for move in MOVES:
            to = peer(move)
            pltpu.make_async_remote_copy(
                src_ref=stage.at[unit, to],
                dst_ref=raw.at[unit, mine],
                send_sem=send_sem.at[unit],
                recv_sem=recv_sem.at[unit],
                device_id=(to, rec),
                device_id_type=MESH,
            ).start()
        local_copy(unit).start()
        raw[unit, 0:TAPS] = jnp.zeros((TAPS, BLOCK), jnp.bfloat16)
        return carry

    for move in MOVES:
        pltpu.make_async_remote_copy(
            src_ref=fir_ref,
            dst_ref=choices.at[me],
            send_sem=fir_send,
            recv_sem=fir_recv,
            device_id=(peer(move), rec),
            device_id_type=MESH,
        ).start()
    choices[me] = fir_ref[...]
    lax.fori_loop(0, UNITS, send_unit, 0)

    def unit_wait(sem, unit):
        count = (NBLK - 1) * SPAN
        pltpu.make_async_copy(
            raw.at[unit, pl.ds(0, count)], raw.at[unit, pl.ds(0, count)], sem.at[unit]
        ).wait()

    def fir_wait(sem):
        view = choices.at[pl.ds(0, NBLK - 1)]
        pltpu.make_async_copy(view, view, sem).wait()

    ownf[0:8] = jnp.zeros((8, BLOCK), jnp.float32)
    unit_wait(recv_sem, 0)
    local_copy(0).wait()

    def store_own(base, rounded, values):
        ownf[pl.ds(base + 8, TAPS)] = values

    inv_own = whiten(raw.at[0], tt_ref, fir_ref[0:1], store_own)

    def shift(d, carry):
        base = pl.multiple_of(d * 128, 128)
        y = ownf[pl.ds(base, 136)] * inv_own
        for lag in range(LAGS):
            row = ((lag // 2) % 2) * 4 + (lag // 4) * 2 + lag % 2
            shifted[row * BLOCK : (row + 1) * BLOCK, pl.ds(base, 128)] = (
                y[8 - lag : 136 - lag].astype(jnp.bfloat16).T
            )
        return carry

    lax.fori_loop(0, TIME // 128, shift, 0, unroll=2)
    fir_wait(fir_recv)

    def store_mate(base, rounded, values):
        mate[pl.ds(base, TAPS)] = rounded

    def half(which):
        rows = pl.ds(pl.multiple_of(which * 4 * BLOCK, BLOCK), 4 * BLOCK)
        return jnp.dot(shifted[rows], mate[...], preferred_element_type=jnp.float32)

    def copy_twin(step):
        return pltpu.make_async_remote_copy(
            src_ref=snd1.at[step],
            dst_ref=rcv1.at[step],
            send_sem=s1_send.at[step],
            recv_sem=s1_recv.at[step],
            device_id=(me, twin),
            device_id_type=MESH,
        )

    def copy_across(step):
        return pltpu.make_async_remote_copy(
            src_ref=snd2.at[step],
            dst_ref=rcv2.at[step],
            send_sem=s2_send.at[step],
            recv_sem=s2_recv.at[step],
            device_id=(me, across),
            device_id_type=MESH,
        )

    def finish(step):
        copy_across(step).wait_recv()
        out_ref[step] = out_ref[step] + rcv2[step].astype(jnp.float32)

    def round_body(step, carry):
        unit_wait(recv_sem, step + 1)
        local_copy(step + 1).wait()
        which = mate_ref[step]
        choice = choices[0]
        for block in range(1, NBLK):
            choice = jnp.where(which == block, choices[block], choice)
        choice = choice[0:1]
        scale = whiten(raw.at[step + 1], tt_ref, choice, store_mate) * (TIME**-0.5)
        snd1[step] = (half(1 - core) * scale).astype(jnp.bfloat16).reshape(2, 2 * BLOCK, BLOCK)
        copy_twin(step).start()
        keep[...] = (half(core) * scale).reshape(2, 2 * BLOCK, BLOCK)
        copy_twin(step).wait_recv()
        snd2[step] = (keep[1 - zlo] + rcv1[step, 1 - zlo].astype(jnp.float32)).astype(jnp.bfloat16)
        copy_across(step).start()
        out_ref[step] = keep[zlo] + rcv1[step, zlo].astype(jnp.float32)

        @pl.when(step > 0)
        def _():
            finish(step - 1)

        return carry

    lax.fori_loop(0, ROUNDS, round_body, 0)
    finish(ROUNDS - 1)
    fir_wait(fir_send)
    for unit in range(UNITS):
        unit_wait(send_sem, unit)
    for step in range(ROUNDS):
        copy_twin(step).wait_send()
        copy_across(step).wait_send()


def prepare_kernel(part_ref, fir_in, bank_ref, rec_ref, stage_ref, fir_ref, mate_ref, tt_ref):
    unit = pl.program_id(0)
    for to in range(NBLK):
        which = jnp.where(unit == 0, to, part_ref[jnp.maximum(unit - 1, 0), to])
        stage_ref[0, to] = rec_ref[:, pl.ds(pl.multiple_of(which * BLOCK, BLOCK), BLOCK)]

    @pl.when(unit == 0)
    def _():
        fir_ref[...] = jnp.broadcast_to(fir_in[...], (8, BLOCK))
        me = lax.axis_index("chan")
        for step in range(ROUNDS):
            mate_ref[step] = jnp.full((8, BLOCK), part_ref[step, me], jnp.int32)
        tap = lax.broadcasted_iota(jnp.int32, (TAPS, 256), 0)
        lane = lax.broadcasted_iota(jnp.int32, (TAPS, 256), 1)
        flip = (tap + lane == TAPS).astype(jnp.float32)
        turned = jnp.dot(
            bank_ref[...], flip, precision=lax.Precision.HIGHEST, preferred_element_type=jnp.float32
        )
        for b in range(BANKS):
            row = jnp.broadcast_to(turned[b : b + 1, :], (TAPS, 256))
            t = pltpu.roll(row, 0, 1, stride=1, stride_axis=0)[:, : 2 * TAPS]
            high = t.astype(jnp.bfloat16)
            low = (t - high.astype(jnp.float32)).astype(jnp.bfloat16)
            tt_ref[b * TAPS : (b + 1) * TAPS, :] = jnp.concatenate([high, low], axis=1)


def prepare(records, fir_choice, bank, partner):
    def whole(*shape):
        return pl.BlockSpec(shape, lambda u, *_: (0,) * len(shape))

    return pl.pallas_call(
        prepare_kernel,
        grid_spec=pltpu.PrefetchScalarGridSpec(
            num_scalar_prefetch=1,
            grid=(UNITS,),
            in_specs=[whole(1, BLOCK), whole(BANKS, TAPS), whole(SPAN, NBLK * BLOCK)],
            out_specs=[
                pl.BlockSpec((1, NBLK, SPAN, BLOCK), lambda u, *_: (u, 0, 0, 0)),
                whole(8, BLOCK),
                whole(ROUNDS, 8, BLOCK),
                whole(BANKS * TAPS, 256),
            ],
        ),
        out_shape=[
            jax.ShapeDtypeStruct((UNITS, NBLK, SPAN, BLOCK), jnp.bfloat16),
            jax.ShapeDtypeStruct((8, BLOCK), jnp.int32),
            jax.ShapeDtypeStruct((ROUNDS, 8, BLOCK), jnp.int32),
            jax.ShapeDtypeStruct((BANKS * TAPS, 256), jnp.bfloat16),
        ],
        compiler_params=pltpu.CompilerParams(vmem_limit_bytes=24 << 20),
        name="prepare",
    )(partner, fir_choice[None, :], bank, records)


def per_device(records, fir_choice, bank, partner):
    ready = prepare(records[0], fir_choice, bank, partner)
    vmem = pl.BlockSpec(memory_space=pltpu.VMEM)
    bf16, f32 = jnp.bfloat16, jnp.float32
    dma = pltpu.SemaphoreType.DMA
    out = pl.pallas_call(
        kernel,
        out_shape=jax.ShapeDtypeStruct((ROUNDS, 2 * BLOCK, BLOCK), f32),
        in_specs=[pl.BlockSpec(memory_space=pl.ANY), vmem, vmem, vmem],
        out_specs=vmem,
        scratch_shapes=[
            pltpu.VMEM((UNITS, TAPS + TIME, BLOCK), bf16),
            pltpu.VMEM((NBLK, 8, BLOCK), jnp.int32),
            pltpu.VMEM((8 + TIME, BLOCK), f32),
            pltpu.VMEM((LAGS * BLOCK, TIME), bf16),
            pltpu.VMEM((TIME, BLOCK), bf16),
            pltpu.VMEM((2, 2 * BLOCK, BLOCK), f32),
            pltpu.VMEM((ROUNDS, 2, 2 * BLOCK, BLOCK), bf16),
            pltpu.VMEM((ROUNDS, 2, 2 * BLOCK, BLOCK), bf16),
            pltpu.VMEM((ROUNDS, 2 * BLOCK, BLOCK), bf16),
            pltpu.VMEM((ROUNDS, 2 * BLOCK, BLOCK), bf16),
            dma((UNITS,)), dma((UNITS,)), dma((UNITS,)), dma, dma,
            dma((ROUNDS,)), dma((ROUNDS,)), dma((ROUNDS,)), dma((ROUNDS,)),
        ],
        compiler_params=pltpu.CompilerParams(
            collective_id=0, has_side_effects=True, vmem_limit_bytes=60 << 20
        ),
        name="correlate",
    )(*ready)
    return out.reshape(ROUNDS, 2, BLOCK, BLOCK).transpose(0, 2, 1, 3)


def solution(mesh):
    placed = (P("rec", "chan", None), P("chan"), P(), P())
    return jax.shard_map(
        per_device,
        mesh=mesh,
        in_specs=placed,
        out_specs=P(None, "chan", "rec", None),
        check_vma=False,
    )
```

```python
import itertools

import jax
import jax.numpy as jnp
from jax import lax
from jax.experimental import pallas as pl
from jax.experimental.pallas import tpu as pltpu
from jax.sharding import PartitionSpec as P

BLOCK = 256
TAPS = 64
LAGS = 8
BANKS = 16
ROUNDS = 3
TIME = 4096
NBLK = 32
SPAN = TIME // NBLK
UNITS = ROUNDS + 1
MESH = pl.DeviceIdType.MESH


def row_pairs():
    groups = []
    for j in range(4):
        dz, dy = j // 2, j % 2
        group = []
        for first, second in ((1, 3), (3, 1), (2, 2), (0, 0)):
            group.append((1 - dz, dy + 2, first))
            group.append((dz, dy, second))
        groups.append(group)
    return groups


GROUPS = row_pairs()
MOVES = [(j, move) for j, group in enumerate(GROUPS) for move in group if move != (0, 0, 0)]


def whiten(raw_ref, tt_ref, choice, ready, store):
    def window(w, acc):
        base = pl.multiple_of(w * TAPS, TAPS)
        x = raw_ref[pl.ds(base, 2 * TAPS), :]
        every = jnp.dot(
            tt_ref[...], jnp.concatenate([x, x], axis=0), preferred_element_type=jnp.float32
        )
        out = every[0:TAPS]
        for b in range(1, BANKS):
            out = jnp.where(choice == b, every[b * TAPS : (b + 1) * TAPS], out)
        rounded = out.astype(jnp.bfloat16)
        values = rounded.astype(jnp.float32)
        store(base, rounded, values)
        return acc + (values * values).reshape(TAPS // 8, 8, BLOCK).sum(0)

    def group(j, acc):
        for row in ready(j):
            for inner in range(1, 8):
                acc = window(row * 8 + inner, acc)
        return acc

    acc = lax.fori_loop(0, len(GROUPS), group, jnp.zeros((8, BLOCK), jnp.float32))
    for row in range(NBLK // 4):
        acc = window(row * 8, acc)
    return lax.rsqrt(acc.sum(0, keepdims=True) * (1.0 / TIME) + 1e-6)


def kernel(
    stage, fir_ref, mate_ref, tt_ref, out_ref,
    raw, choices, ownf, shifted, mate, keep, snd1, rcv1, snd2, rcv2,
    send_sem, recv_sem, local_sem, fir_send, fir_recv, s1_send, s1_recv, s2_send, s2_recv,
):
    me = lax.axis_index("chan")
    rec = lax.axis_index("rec")
    mz, my, mx = me // 16, (me // 4) % 4, me % 4
    core, zlo = rec % 2, rec // 2
    twin = zlo * 2 + (1 - core)
    across = (1 - zlo) * 2 + core

    turn = 1 - 2 * core

    def peer(move):
        dz, dy, dx = move
        return ((mz + dz) % 2) * 16 + ((my + 4 + turn * dy) % 4) * 4 + (mx + 4 + turn * dx) % 4

    barrier = pltpu.get_barrier_semaphore()
    for _, move in MOVES:
        pl.semaphore_signal(barrier, inc=1, device_id=(peer(move), rec), device_id_type=MESH)
    pl.semaphore_signal(barrier, inc=1, device_id=(me, twin), device_id_type=MESH)
    pl.semaphore_signal(barrier, inc=1, device_id=(me, across), device_id_type=MESH)
    pl.semaphore_wait(barrier, len(MOVES) + 2)

    mine = pl.ds(pl.multiple_of(TAPS + me * SPAN, TAPS), SPAN)

    def local_copy(unit):
        return pltpu.make_async_copy(stage.at[unit, me], raw.at[unit, mine], local_sem.at[unit])

    def send_unit(unit, carry):
        for j, move in MOVES:
            to = peer(move)
            pltpu.make_async_remote_copy(
                src_ref=stage.at[unit, to],
                dst_ref=raw.at[unit, mine],
                send_sem=send_sem.at[unit],
                recv_sem=recv_sem.at[unit, j],
                device_id=(to, rec),
                device_id_type=MESH,
            ).start()
        local_copy(unit).start()
        raw[unit, 0:TAPS] = jnp.zeros((TAPS, BLOCK), jnp.bfloat16)
        return carry

    for _, move in MOVES:
        pltpu.make_async_remote_copy(
            src_ref=fir_ref,
            dst_ref=choices.at[me],
            send_sem=fir_send,
            recv_sem=fir_recv,
            device_id=(peer(move), rec),
            device_id_type=MESH,
        ).start()
    choices[me] = fir_ref[...]
    lax.fori_loop(0, UNITS, send_unit, 0)

    def bytes_wait(sem, pieces):
        view = raw.at[0, pl.ds(0, pieces * SPAN)]
        pltpu.make_async_copy(view, view, sem).wait()

    def arrival(unit):
        def ready(j):
            dz, dy = j // 2, j % 2

            @pl.when(j == 0)
            def _():
                bytes_wait(recv_sem.at[unit, j], 7)
                local_copy(unit).wait()

            @pl.when(j > 0)
            def _():
                bytes_wait(recv_sem.at[unit, j], 8)

            first = ((mz + dz) % 2) * 4 + (my + 4 - turn * dy) % 4
            second = ((mz + 1 - dz) % 2) * 4 + (my + 8 - turn * (dy + 2)) % 4
            return first, second

        return ready

    def fir_wait(sem):
        view = choices.at[pl.ds(0, NBLK - 1)]
        pltpu.make_async_copy(view, view, sem).wait()

    ownf[0:8] = jnp.zeros((8, BLOCK), jnp.float32)

    def store_own(base, rounded, values):
        ownf[pl.ds(base + 8, TAPS)] = values

    inv_own = whiten(raw.at[0], tt_ref, fir_ref[0:1], arrival(0), store_own)

    def shift(d, carry):
        base = pl.multiple_of(d * 128, 128)
        y = ownf[pl.ds(base, 136)] * inv_own
        for lag in range(LAGS):
            row = ((lag // 2) % 2) * 4 + (lag // 4) * 2 + lag % 2
            shifted[row * BLOCK : (row + 1) * BLOCK, pl.ds(base, 128)] = (
                y[8 - lag : 136 - lag].astype(jnp.bfloat16).T
            )
        return carry

    lax.fori_loop(0, TIME // 128, shift, 0, unroll=2)
    fir_wait(fir_recv)

    def store_mate(base, rounded, values):
        mate[pl.ds(base, TAPS)] = rounded

    def quarter(to_core, to_zlo):
        rows = pl.ds(pl.multiple_of((to_core * 2 + to_zlo) * 2 * BLOCK, BLOCK), 2 * BLOCK)
        return jnp.dot(shifted[rows], mate[...], preferred_element_type=jnp.float32)

    def copy_twin(step, part):
        return pltpu.make_async_remote_copy(
            src_ref=snd1.at[step, part],
            dst_ref=rcv1.at[step, part],
            send_sem=s1_send.at[step, part],
            recv_sem=s1_recv.at[step, part],
            device_id=(me, twin),
            device_id_type=MESH,
        )

    def copy_across(step):
        return pltpu.make_async_remote_copy(
            src_ref=snd2.at[step],
            dst_ref=rcv2.at[step],
            send_sem=s2_send.at[step],
            recv_sem=s2_recv.at[step],
            device_id=(me, across),
            device_id_type=MESH,
        )

    def finish(step):
        copy_across(step).wait_recv()
        out_ref[step] = out_ref[step] + rcv2[step].astype(jnp.float32)

    def round_body(step, carry):
        which = mate_ref[step]
        choice = choices[0]
        for block in range(1, NBLK):
            choice = jnp.where(which == block, choices[block], choice)
        choice = choice[0:1]
        inv = whiten(raw.at[step + 1], tt_ref, choice, arrival(step + 1), store_mate)
        scale = inv * (TIME**-0.5)
        for part, target in ((0, 1 - zlo), (1, zlo)):
            snd1[step, part] = (quarter(1 - core, target) * scale).astype(jnp.bfloat16)
            copy_twin(step, part).start()
            keep[...] = quarter(core, target) * scale
            copy_twin(step, part).wait_recv()
            both = keep[...] + rcv1[step, part].astype(jnp.float32)
            if part == 0:
                snd2[step] = both.astype(jnp.bfloat16)
                copy_across(step).start()
            else:
                out_ref[step] = both

        @pl.when(step > 0)
        def _():
            finish(step - 1)

        return carry

    lax.fori_loop(0, ROUNDS, round_body, 0)
    finish(ROUNDS - 1)
    fir_wait(fir_send)
    for unit in range(UNITS):
        bytes_wait(send_sem.at[unit], NBLK - 1)
    for step in range(ROUNDS):
        copy_twin(step, 0).wait_send()
        copy_twin(step, 1).wait_send()
        copy_across(step).wait_send()


def prepare_kernel(
    part_hbm, fir_hbm, bank_hbm, rec_hbm, stage_ref, fir_ref, mate_ref, tt_ref,
    part_ref, fir_in, bank_ref, rec_ref, sem, rec_sem,
):
    slices = rec_sem.shape[0]
    rows = SPAN // slices
    small = [
        pltpu.make_async_copy(source, target, sem.at[i])
        for i, (source, target) in enumerate(
            ((part_hbm, part_ref), (bank_hbm, bank_ref), (fir_hbm, fir_in))
        )
    ]
    large = [
        pltpu.make_async_copy(
            rec_hbm.at[pl.ds(i * rows, rows)], rec_ref.at[pl.ds(i * rows, rows)], rec_sem.at[i]
        )
        for i in range(slices)
    ]
    for copy in small + large:
        copy.start()
    for copy in small:
        copy.wait()

    fir_ref[...] = jnp.broadcast_to(fir_in[...], (8, BLOCK))
    me = lax.axis_index("chan")
    for step in range(ROUNDS):
        mate_ref[step] = jnp.full((8, BLOCK), part_ref[step, me], jnp.int32)
    tap = lax.broadcasted_iota(jnp.int32, (TAPS, 256), 0)
    lane = lax.broadcasted_iota(jnp.int32, (TAPS, 256), 1)
    flip = (tap + lane == TAPS).astype(jnp.float32)
    turned = jnp.dot(
        bank_ref[...], flip, precision=lax.Precision.HIGHEST, preferred_element_type=jnp.float32
    )
    for b in range(BANKS):
        row = jnp.broadcast_to(turned[b : b + 1, :], (TAPS, 256))
        t = pltpu.roll(row, 0, 1, stride=1, stride_axis=0)[:, : 2 * TAPS]
        high = t.astype(jnp.bfloat16)
        low = (t - high.astype(jnp.float32)).astype(jnp.bfloat16)
        tt_ref[b * TAPS : (b + 1) * TAPS, :] = jnp.concatenate([high, low], axis=1)

    for i in range(slices):
        large[i].wait()
        cut = slice(i * rows, (i + 1) * rows)
        for to in range(NBLK):
            stage_ref[0, to, cut] = rec_ref[cut, to * BLOCK : (to + 1) * BLOCK]
            for step in range(ROUNDS):
                start = pl.multiple_of(part_ref[step, to] * BLOCK, BLOCK)
                stage_ref[step + 1, to, cut] = rec_ref[cut, pl.ds(start, BLOCK)]


def prepare(records, fir_choice, bank, partner):
    hbm = pl.BlockSpec(memory_space=pltpu.HBM)
    vmem = pl.BlockSpec(memory_space=pltpu.VMEM)
    slices = 2
    return pl.pallas_call(
        prepare_kernel,
        in_specs=[hbm] * 4,
        out_specs=[vmem] * 4,
        out_shape=[
            jax.ShapeDtypeStruct((UNITS, NBLK, SPAN, BLOCK), jnp.bfloat16),
            jax.ShapeDtypeStruct((8, BLOCK), jnp.int32),
            jax.ShapeDtypeStruct((ROUNDS, 8, BLOCK), jnp.int32),
            jax.ShapeDtypeStruct((BANKS * TAPS, 256), jnp.bfloat16),
        ],
        scratch_shapes=[
            pltpu.SMEM((ROUNDS, NBLK), jnp.int32),
            pltpu.VMEM((1, BLOCK), jnp.int32),
            pltpu.VMEM((BANKS, TAPS), jnp.float32),
            pltpu.VMEM((SPAN, NBLK * BLOCK), jnp.bfloat16),
            pltpu.SemaphoreType.DMA((3,)),
            pltpu.SemaphoreType.DMA((slices,)),
        ],
        compiler_params=pltpu.CompilerParams(vmem_limit_bytes=14 << 20),
        name="prepare",
    )(partner, fir_choice[None, :], bank, records)


def per_device(records, fir_choice, bank, partner):
    ready = prepare(records[0], fir_choice, bank, partner)
    vmem = pl.BlockSpec(memory_space=pltpu.VMEM)
    bf16, f32 = jnp.bfloat16, jnp.float32
    dma = pltpu.SemaphoreType.DMA
    out = pl.pallas_call(
        kernel,
        out_shape=jax.ShapeDtypeStruct((ROUNDS, 2 * BLOCK, BLOCK), f32),
        in_specs=[pl.BlockSpec(memory_space=pl.ANY), vmem, vmem, vmem],
        out_specs=vmem,
        scratch_shapes=[
            pltpu.VMEM((UNITS, TAPS + TIME, BLOCK), bf16),
            pltpu.VMEM((NBLK, 8, BLOCK), jnp.int32),
            pltpu.VMEM((8 + TIME, BLOCK), f32),
            pltpu.VMEM((LAGS * BLOCK, TIME), bf16),
            pltpu.VMEM((TIME, BLOCK), bf16),
            pltpu.VMEM((2 * BLOCK, BLOCK), f32),
            pltpu.VMEM((ROUNDS, 2, 2 * BLOCK, BLOCK), bf16),
            pltpu.VMEM((ROUNDS, 2, 2 * BLOCK, BLOCK), bf16),
            pltpu.VMEM((ROUNDS, 2 * BLOCK, BLOCK), bf16),
            pltpu.VMEM((ROUNDS, 2 * BLOCK, BLOCK), bf16),
            dma((UNITS,)), dma((UNITS, len(GROUPS))), dma((UNITS,)), dma, dma,
            dma((ROUNDS, 2)), dma((ROUNDS, 2)), dma((ROUNDS,)), dma((ROUNDS,)),
        ],
        compiler_params=pltpu.CompilerParams(
            collective_id=0, has_side_effects=True, vmem_limit_bytes=40 << 20
        ),
        name="correlate",
    )(*ready)
    return out.reshape(ROUNDS, 2, BLOCK, BLOCK).transpose(0, 2, 1, 3)


def solution(mesh):
    placed = (P("rec", "chan", None), P("chan"), P(), P())
    return jax.shard_map(
        per_device,
        mesh=mesh,
        in_specs=placed,
        out_specs=P(None, "chan", "rec", None),
        check_vma=False,
    )
```

```python
import itertools

import jax
import jax.numpy as jnp
from jax import lax
from jax.experimental import pallas as pl
from jax.experimental.pallas import tpu as pltpu
from jax.sharding import PartitionSpec as P

BLOCK = 256
TAPS = 64
LAGS = 8
BANKS = 16
ROUNDS = 3
TIME = 4096
NBLK = 32
SPAN = TIME // NBLK
UNITS = ROUNDS + 1
MESH = pl.DeviceIdType.MESH


def row_pairs():
    groups = []
    for j in range(4):
        dz, dy = j // 2, j % 2
        group = []
        for first, second in ((1, 3), (3, 1), (2, 2), (0, 0)):
            group.append((1 - dz, dy + 2, first))
            group.append((dz, dy, second))
        groups.append(group)
    return groups


GROUPS = row_pairs()
MOVES = [(j, move) for j, group in enumerate(GROUPS) for move in group if move != (0, 0, 0)]


def whiten(raw_ref, tt_ref, choice, ready, store):
    def window(w, acc):
        base = pl.multiple_of(w * TAPS, TAPS)
        x = raw_ref[pl.ds(base, 2 * TAPS), :]
        every = jnp.dot(
            tt_ref[...], jnp.concatenate([x, x], axis=0), preferred_element_type=jnp.float32
        )
        out = every[0:TAPS]
        for b in range(1, BANKS):
            out = jnp.where(choice == b, every[b * TAPS : (b + 1) * TAPS], out)
        rounded = out.astype(jnp.bfloat16)
        values = rounded.astype(jnp.float32)
        store(base, rounded, values)
        return acc + (values * values).reshape(TAPS // 8, 8, BLOCK).sum(0)

    def group(j, acc):
        for row in ready(j):
            for inner in range(1, 8):
                acc = window(row * 8 + inner, acc)
        return acc

    acc = lax.fori_loop(0, len(GROUPS), group, jnp.zeros((8, BLOCK), jnp.float32))
    for row in range(NBLK // 4):
        acc = window(row * 8, acc)
    return lax.rsqrt(acc.sum(0, keepdims=True) * (1.0 / TIME) + 1e-6)


def kernel(
    stage, fir_ref, mate_ref, tt_ref, out_ref,
    raw, choices, ownf, shifted, mate, keep, snd1, rcv1, snd2, rcv2,
    send_sem, recv_sem, local_sem, fir_send, fir_recv, s1_send, s1_recv, s2_send, s2_recv,
):
    me = lax.axis_index("chan")
    rec = lax.axis_index("rec")
    mz, my, mx = me // 16, (me // 4) % 4, me % 4
    core, zlo = rec % 2, rec // 2
    twin = zlo * 2 + (1 - core)
    across = (1 - zlo) * 2 + core

    turn = 1 - 2 * core

    def peer(move):
        dz, dy, dx = move
        return ((mz + dz) % 2) * 16 + ((my + 4 + turn * dy) % 4) * 4 + (mx + 4 + turn * dx) % 4

    barrier = pltpu.get_barrier_semaphore()
    for _, move in MOVES:
        pl.semaphore_signal(barrier, inc=1, device_id=(peer(move), rec), device_id_type=MESH)
    pl.semaphore_signal(barrier, inc=1, device_id=(me, twin), device_id_type=MESH)
    pl.semaphore_signal(barrier, inc=1, device_id=(me, across), device_id_type=MESH)
    pl.semaphore_wait(barrier, len(MOVES) + 2)

    mine = pl.ds(pl.multiple_of(TAPS + me * SPAN, TAPS), SPAN)

    def local_copy(unit):
        return pltpu.make_async_copy(stage.at[unit, me], raw.at[unit, mine], local_sem.at[unit])

    def send_unit(unit, carry):
        for j, move in MOVES:
            to = peer(move)
            pltpu.make_async_remote_copy(
                src_ref=stage.at[unit, to],
                dst_ref=raw.at[unit, mine],
                send_sem=send_sem.at[unit],
                recv_sem=recv_sem.at[unit, j],
                device_id=(to, rec),
                device_id_type=MESH,
            ).start()
        local_copy(unit).start()
        raw[unit, 0:TAPS] = jnp.zeros((TAPS, BLOCK), jnp.bfloat16)
        return carry

    send_unit(0, 0)
    for _, move in MOVES:
        pltpu.make_async_remote_copy(
            src_ref=fir_ref,
            dst_ref=choices.at[me],
            send_sem=fir_send,
            recv_sem=fir_recv,
            device_id=(peer(move), rec),
            device_id_type=MESH,
        ).start()
    choices[me] = fir_ref[...]
    lax.fori_loop(1, UNITS, send_unit, 0)

    def bytes_wait(sem, pieces):
        view = raw.at[0, pl.ds(0, pieces * SPAN)]
        pltpu.make_async_copy(view, view, sem).wait()

    def arrival(unit):
        def ready(j):
            dz, dy = j // 2, j % 2

            @pl.when(j == 0)
            def _():
                bytes_wait(recv_sem.at[unit, j], 7)
                local_copy(unit).wait()

            @pl.when(j > 0)
            def _():
                bytes_wait(recv_sem.at[unit, j], 8)

            first = ((mz + dz) % 2) * 4 + (my + 4 - turn * dy) % 4
            second = ((mz + 1 - dz) % 2) * 4 + (my + 8 - turn * (dy + 2)) % 4
            return first, second

        return ready

    def fir_wait(sem):
        view = choices.at[pl.ds(0, NBLK - 1)]
        pltpu.make_async_copy(view, view, sem).wait()

    ownf[0:8] = jnp.zeros((8, BLOCK), jnp.float32)

    def store_own(base, rounded, values):
        ownf[pl.ds(base + 8, TAPS)] = values

    inv_own = whiten(raw.at[0], tt_ref, fir_ref[0:1], arrival(0), store_own)

    def shift(d, carry):
        base = pl.multiple_of(d * 128, 128)
        y = ownf[pl.ds(base, 136)] * inv_own
        for lag in range(LAGS):
            row = ((lag // 2) % 2) * 4 + (lag // 4) * 2 + lag % 2
            shifted[row * BLOCK : (row + 1) * BLOCK, pl.ds(base, 128)] = (
                y[8 - lag : 136 - lag].astype(jnp.bfloat16).T
            )
        return carry

    lax.fori_loop(0, TIME // 128, shift, 0, unroll=2)
    fir_wait(fir_recv)

    def store_mate(base, rounded, values):
        mate[pl.ds(base, TAPS)] = rounded

    def product(to_core, to_zlo, first, count):
        start = ((to_core * 2 + to_zlo) * 2 + first) * BLOCK
        rows = pl.ds(pl.multiple_of(start, BLOCK), count * BLOCK)
        return jnp.dot(shifted[rows], mate[...], preferred_element_type=jnp.float32)

    def copy_twin(step, part):
        if part == 2:
            where = (step, 1)
        else:
            where = (step, 0, pl.ds(part * BLOCK, BLOCK))
        return pltpu.make_async_remote_copy(
            src_ref=snd1.at[where],
            dst_ref=rcv1.at[where],
            send_sem=s1_send.at[step, part],
            recv_sem=s1_recv.at[step, part],
            device_id=(me, twin),
            device_id_type=MESH,
        )

    def copy_across(step, lag):
        where = (step, pl.ds(lag * BLOCK, BLOCK))
        return pltpu.make_async_remote_copy(
            src_ref=snd2.at[where],
            dst_ref=rcv2.at[where],
            send_sem=s2_send.at[step, lag],
            recv_sem=s2_recv.at[step, lag],
            device_id=(me, across),
            device_id_type=MESH,
        )

    def finish(step):
        for lag in range(2):
            here = slice(lag * BLOCK, (lag + 1) * BLOCK)
            copy_across(step, lag).wait_recv()
            out_ref[step, here] = out_ref[step, here] + rcv2[step, here].astype(jnp.float32)

    def round_body(step, carry):
        which = mate_ref[step]
        choice = choices[0]
        for block in range(1, NBLK):
            choice = jnp.where(which == block, choices[block], choice)
        choice = choice[0:1]
        inv = whiten(raw.at[step + 1], tt_ref, choice, arrival(step + 1), store_mate)
        scale = inv * (TIME**-0.5)
        for lag in range(2):
            here = slice(lag * BLOCK, (lag + 1) * BLOCK)
            away = product(1 - core, 1 - zlo, lag, 1) * scale
            snd1[step, 0, here] = away.astype(jnp.bfloat16)
            copy_twin(step, lag).start()
        for lag in range(2):
            here = slice(lag * BLOCK, (lag + 1) * BLOCK)
            keep[here] = product(core, 1 - zlo, lag, 1) * scale
            copy_twin(step, lag).wait_recv()
            both = keep[here] + rcv1[step, 0, here].astype(jnp.float32)
            snd2[step, here] = both.astype(jnp.bfloat16)
            copy_across(step, lag).start()
        snd1[step, 1] = (product(1 - core, zlo, 0, 2) * scale).astype(jnp.bfloat16)
        copy_twin(step, 2).start()
        keep[...] = product(core, zlo, 0, 2) * scale
        copy_twin(step, 2).wait_recv()
        out_ref[step] = keep[...] + rcv1[step, 1].astype(jnp.float32)

        @pl.when(step > 0)
        def _():
            finish(step - 1)

        return carry

    lax.fori_loop(0, ROUNDS, round_body, 0)
    finish(ROUNDS - 1)
    fir_wait(fir_send)
    for unit in range(UNITS):
        bytes_wait(send_sem.at[unit], NBLK - 1)
    for step in range(ROUNDS):
        for part in range(3):
            copy_twin(step, part).wait_send()
        for lag in range(2):
            copy_across(step, lag).wait_send()


def prepare_kernel(
    small_hbm, bank_hbm, rec_hbm, stage_ref, fir_ref, mate_ref, tt_ref,
    part_ref, small_ref, bank_ref, rec_ref, sem, rec_sem,
):
    slices = rec_sem.shape[0]
    rows = SPAN // slices
    small = [
        pltpu.make_async_copy(source, target, sem.at[i])
        for i, (source, target) in enumerate(
            ((small_hbm, part_ref), (bank_hbm, bank_ref), (small_hbm, small_ref))
        )
    ]
    large = [
        pltpu.make_async_copy(
            rec_hbm.at[pl.ds(i * rows, rows)], rec_ref.at[pl.ds(i * rows, rows)], rec_sem.at[i]
        )
        for i in range(slices)
    ]
    for copy in small + large:
        copy.start()
    for copy in small:
        copy.wait()

    fir_ref[...] = jnp.broadcast_to(small_ref[ROUNDS : ROUNDS + 1, :], (8, BLOCK))
    me = lax.axis_index("chan")
    for step in range(ROUNDS):
        mate_ref[step] = jnp.full((8, BLOCK), part_ref[step, me], jnp.int32)
    tap = lax.broadcasted_iota(jnp.int32, (TAPS, 256), 0)
    lane = lax.broadcasted_iota(jnp.int32, (TAPS, 256), 1)
    flip = (tap + lane == TAPS).astype(jnp.float32)
    turned = jnp.dot(
        bank_ref[...], flip, precision=lax.Precision.HIGHEST, preferred_element_type=jnp.float32
    )
    for b in range(BANKS):
        row = jnp.broadcast_to(turned[b : b + 1, :], (TAPS, 256))
        t = pltpu.roll(row, 0, 1, stride=1, stride_axis=0)[:, : 2 * TAPS]
        high = t.astype(jnp.bfloat16)
        low = (t - high.astype(jnp.float32)).astype(jnp.bfloat16)
        tt_ref[b * TAPS : (b + 1) * TAPS, :] = jnp.concatenate([high, low], axis=1)

    for i in range(slices):
        large[i].wait()
        cut = slice(i * rows, (i + 1) * rows)
        for to in range(NBLK):
            stage_ref[0, to, cut] = rec_ref[cut, to * BLOCK : (to + 1) * BLOCK]
            for step in range(ROUNDS):
                start = pl.multiple_of(part_ref[step, to] * BLOCK, BLOCK)
                stage_ref[step + 1, to, cut] = rec_ref[cut, pl.ds(start, BLOCK)]


def prepare(records, fir_choice, bank, partner):
    hbm = pl.BlockSpec(memory_space=pltpu.HBM)
    vmem = pl.BlockSpec(memory_space=pltpu.VMEM)
    slices = 2
    small = jnp.concatenate(
        [
            jnp.pad(partner, ((0, 0), (0, BLOCK - NBLK))),
            jnp.pad(fir_choice[None, :], ((0, 8 - ROUNDS - 1), (0, 0))),
        ],
        axis=0,
    )
    return pl.pallas_call(
        prepare_kernel,
        in_specs=[hbm] * 3,
        out_specs=[vmem] * 4,
        out_shape=[
            jax.ShapeDtypeStruct((UNITS, NBLK, SPAN, BLOCK), jnp.bfloat16),
            jax.ShapeDtypeStruct((8, BLOCK), jnp.int32),
            jax.ShapeDtypeStruct((ROUNDS, 8, BLOCK), jnp.int32),
            jax.ShapeDtypeStruct((BANKS * TAPS, 256), jnp.bfloat16),
        ],
        scratch_shapes=[
            pltpu.SMEM((8, BLOCK), jnp.int32),
            pltpu.VMEM((8, BLOCK), jnp.int32),
            pltpu.VMEM((BANKS, TAPS), jnp.float32),
            pltpu.VMEM((SPAN, NBLK * BLOCK), jnp.bfloat16),
            pltpu.SemaphoreType.DMA((3,)),
            pltpu.SemaphoreType.DMA((slices,)),
        ],
        compiler_params=pltpu.CompilerParams(vmem_limit_bytes=14 << 20),
        name="prepare",
    )(small, bank, records)


def per_device(records, fir_choice, bank, partner):
    ready = prepare(records[0], fir_choice, bank, partner)
    vmem = pl.BlockSpec(memory_space=pltpu.VMEM)
    bf16, f32 = jnp.bfloat16, jnp.float32
    dma = pltpu.SemaphoreType.DMA
    out = pl.pallas_call(
        kernel,
        out_shape=jax.ShapeDtypeStruct((ROUNDS, 2 * BLOCK, BLOCK), f32),
        in_specs=[pl.BlockSpec(memory_space=pl.ANY), vmem, vmem, vmem],
        out_specs=vmem,
        scratch_shapes=[
            pltpu.VMEM((UNITS, TAPS + TIME, BLOCK), bf16),
            pltpu.VMEM((NBLK, 8, BLOCK), jnp.int32),
            pltpu.VMEM((8 + TIME, BLOCK), f32),
            pltpu.VMEM((LAGS * BLOCK, TIME), bf16),
            pltpu.VMEM((TIME, BLOCK), bf16),
            pltpu.VMEM((2 * BLOCK, BLOCK), f32),
            pltpu.VMEM((ROUNDS, 2, 2 * BLOCK, BLOCK), bf16),
            pltpu.VMEM((ROUNDS, 2, 2 * BLOCK, BLOCK), bf16),
            pltpu.VMEM((ROUNDS, 2 * BLOCK, BLOCK), bf16),
            pltpu.VMEM((ROUNDS, 2 * BLOCK, BLOCK), bf16),
            dma((UNITS,)), dma((UNITS, len(GROUPS))), dma((UNITS,)), dma, dma,
            dma((ROUNDS, 3)), dma((ROUNDS, 3)), dma((ROUNDS, 2)), dma((ROUNDS, 2)),
        ],
        compiler_params=pltpu.CompilerParams(
            collective_id=0, has_side_effects=True, vmem_limit_bytes=40 << 20
        ),
        name="correlate",
    )(*ready)
    return out.reshape(ROUNDS, 2, BLOCK, BLOCK).transpose(0, 2, 1, 3)


def solution(mesh):
    placed = (P("rec", "chan", None), P("chan"), P(), P())
    return jax.shard_map(
        per_device,
        mesh=mesh,
        in_specs=placed,
        out_specs=P(None, "chan", "rec", None),
        check_vma=False,
    )
```

```python
import itertools

import jax
import jax.numpy as jnp
from jax import lax
from jax.experimental import pallas as pl
from jax.experimental.pallas import tpu as pltpu
from jax.sharding import PartitionSpec as P

BLOCK = 256
TAPS = 64
LAGS = 8
BANKS = 16
ROUNDS = 3
TIME = 4096
NBLK = 32
SPAN = TIME // NBLK
UNITS = ROUNDS + 1
MESH = pl.DeviceIdType.MESH


def row_pairs():
    groups = []
    for j in range(4):
        dz, dy = j // 2, j % 2
        group = []
        for first, second in ((1, 3), (3, 1), (2, 2), (0, 0)):
            group.append((1 - dz, dy + 2, first))
            group.append((dz, dy, second))
        groups.append(group)
    return groups


GROUPS = row_pairs()
MOVES = [(j, move) for j, group in enumerate(GROUPS) for move in group if move != (0, 0, 0)]


def whiten(raw_ref, tt_ref, choice, ready, store):
    def window(w, acc):
        base = pl.multiple_of(w * TAPS, TAPS)
        x = raw_ref[pl.ds(base, 2 * TAPS), :]
        every = jnp.dot(
            tt_ref[...], jnp.concatenate([x, x], axis=0), preferred_element_type=jnp.float32
        )
        out = every[0:TAPS]
        for b in range(1, BANKS):
            out = jnp.where(choice == b, every[b * TAPS : (b + 1) * TAPS], out)
        rounded = out.astype(jnp.bfloat16)
        values = rounded.astype(jnp.float32)
        store(base, rounded, values)
        return acc + (values * values).reshape(TAPS // 8, 8, BLOCK).sum(0)

    def group(j, acc):
        for row in ready(j):
            for inner in range(1, 8):
                acc = window(row * 8 + inner, acc)
        return acc

    acc = lax.fori_loop(0, len(GROUPS), group, jnp.zeros((8, BLOCK), jnp.float32))
    for row in range(NBLK // 4):
        acc = window(row * 8, acc)
    return lax.rsqrt(acc.sum(0, keepdims=True) * (1.0 / TIME) + 1e-6)


def kernel(
    stage, fir_ref, mate_ref, tt_ref, out_ref,
    raw, choices, ownf, shifted, mate, keep, snd1, rcv1, snd2, rcv2,
    send_sem, recv_sem, local_sem, fir_send, fir_recv, s1_send, s1_recv, s2_send, s2_recv,
):
    me = lax.axis_index("chan")
    rec = lax.axis_index("rec")
    mz, my, mx = me // 16, (me // 4) % 4, me % 4
    core, zlo = rec % 2, rec // 2
    twin = zlo * 2 + (1 - core)
    across = (1 - zlo) * 2 + core

    turn = 1 - 2 * core

    def peer(move):
        dz, dy, dx = move
        return ((mz + dz) % 2) * 16 + ((my + 4 + turn * dy) % 4) * 4 + (mx + 4 + turn * dx) % 4

    barrier = pltpu.get_barrier_semaphore()
    for _, move in MOVES:
        pl.semaphore_signal(barrier, inc=1, device_id=(peer(move), rec), device_id_type=MESH)
    pl.semaphore_signal(barrier, inc=1, device_id=(me, twin), device_id_type=MESH)
    pl.semaphore_signal(barrier, inc=1, device_id=(me, across), device_id_type=MESH)
    pl.semaphore_wait(barrier, len(MOVES) + 2)

    mine = pl.ds(pl.multiple_of(TAPS + me * SPAN, TAPS), SPAN)

    def local_copy(unit):
        return pltpu.make_async_copy(stage.at[unit, me], raw.at[unit, mine], local_sem.at[unit])

    def send_unit(unit, carry):
        for j, move in MOVES:
            to = peer(move)
            pltpu.make_async_remote_copy(
                src_ref=stage.at[unit, to],
                dst_ref=raw.at[unit, mine],
                send_sem=send_sem.at[unit],
                recv_sem=recv_sem.at[unit, j],
                device_id=(to, rec),
                device_id_type=MESH,
            ).start()
        local_copy(unit).start()
        raw[unit, 0:TAPS] = jnp.zeros((TAPS, BLOCK), jnp.bfloat16)
        return carry

    send_unit(0, 0)
    for _, move in MOVES:
        pltpu.make_async_remote_copy(
            src_ref=fir_ref,
            dst_ref=choices.at[me],
            send_sem=fir_send,
            recv_sem=fir_recv,
            device_id=(peer(move), rec),
            device_id_type=MESH,
        ).start()
    choices[me] = fir_ref[...]
    lax.fori_loop(1, UNITS - 1, send_unit, 0)

    def bytes_wait(sem, pieces):
        view = raw.at[0, pl.ds(0, pieces * SPAN)]
        pltpu.make_async_copy(view, view, sem).wait()

    def arrival(unit):
        def ready(j):
            dz, dy = j // 2, j % 2

            @pl.when(j == 0)
            def _():
                bytes_wait(recv_sem.at[unit, j], 7)
                local_copy(unit).wait()

            @pl.when(j > 0)
            def _():
                bytes_wait(recv_sem.at[unit, j], 8)

            first = ((mz + dz) % 2) * 4 + (my + 4 - turn * dy) % 4
            second = ((mz + 1 - dz) % 2) * 4 + (my + 8 - turn * (dy + 2)) % 4
            return first, second

        return ready

    def fir_wait(sem):
        view = choices.at[pl.ds(0, NBLK - 1)]
        pltpu.make_async_copy(view, view, sem).wait()

    ownf[0:8] = jnp.zeros((8, BLOCK), jnp.float32)

    def store_own(base, rounded, values):
        ownf[pl.ds(base + 8, TAPS)] = values

    inv_own = whiten(raw.at[0], tt_ref, fir_ref[0:1], arrival(0), store_own)
    send_unit(UNITS - 1, 0)

    def shift(d, carry):
        base = pl.multiple_of(d * 128, 128)
        y = ownf[pl.ds(base, 136)] * inv_own
        for lag in range(LAGS):
            row = ((lag // 2) % 2) * 4 + (lag // 4) * 2 + lag % 2
            shifted[row * BLOCK : (row + 1) * BLOCK, pl.ds(base, 128)] = (
                y[8 - lag : 136 - lag].astype(jnp.bfloat16).T
            )
        return carry

    lax.fori_loop(0, TIME // 128, shift, 0, unroll=2)
    fir_wait(fir_recv)

    def store_mate(base, rounded, values):
        mate[pl.ds(base, TAPS)] = rounded

    def product(to_core, to_zlo, first, count):
        start = ((to_core * 2 + to_zlo) * 2 + first) * BLOCK
        rows = pl.ds(pl.multiple_of(start, BLOCK), count * BLOCK)
        return jnp.dot(shifted[rows], mate[...], preferred_element_type=jnp.float32)

    def copy_twin(step, part):
        if part == 2:
            where = (step, 1)
        else:
            where = (step, 0, pl.ds(part * BLOCK, BLOCK))
        return pltpu.make_async_remote_copy(
            src_ref=snd1.at[where],
            dst_ref=rcv1.at[where],
            send_sem=s1_send.at[step, part],
            recv_sem=s1_recv.at[step, part],
            device_id=(me, twin),
            device_id_type=MESH,
        )

    def copy_across(step, lag):
        where = (step, pl.ds(lag * BLOCK, BLOCK))
        return pltpu.make_async_remote_copy(
            src_ref=snd2.at[where],
            dst_ref=rcv2.at[where],
            send_sem=s2_send.at[step, lag],
            recv_sem=s2_recv.at[step, lag],
            device_id=(me, across),
            device_id_type=MESH,
        )

    def finish(step):
        for lag in range(2):
            here = slice(lag * BLOCK, (lag + 1) * BLOCK)
            copy_across(step, lag).wait_recv()
            out_ref[step, here] = out_ref[step, here] + rcv2[step, here].astype(jnp.float32)

    def round_body(step, carry):
        which = mate_ref[step]
        choice = choices[0]
        for block in range(1, NBLK):
            choice = jnp.where(which == block, choices[block], choice)
        choice = choice[0:1]
        inv = whiten(raw.at[step + 1], tt_ref, choice, arrival(step + 1), store_mate)
        scale = inv * (TIME**-0.5)
        for lag in range(2):
            here = slice(lag * BLOCK, (lag + 1) * BLOCK)
            away = product(1 - core, 1 - zlo, lag, 1) * scale
            snd1[step, 0, here] = away.astype(jnp.bfloat16)
            copy_twin(step, lag).start()
        for lag in range(2):
            here = slice(lag * BLOCK, (lag + 1) * BLOCK)
            keep[here] = product(core, 1 - zlo, lag, 1) * scale
            copy_twin(step, lag).wait_recv()
            both = keep[here] + rcv1[step, 0, here].astype(jnp.float32)
            snd2[step, here] = both.astype(jnp.bfloat16)
            copy_across(step, lag).start()
        snd1[step, 1] = (product(1 - core, zlo, 0, 2) * scale).astype(jnp.bfloat16)
        copy_twin(step, 2).start()
        keep[...] = product(core, zlo, 0, 2) * scale
        copy_twin(step, 2).wait_recv()
        out_ref[step] = keep[...] + rcv1[step, 1].astype(jnp.float32)

        @pl.when(step > 0)
        def _():
            finish(step - 1)

        return carry

    lax.fori_loop(0, ROUNDS, round_body, 0)
    finish(ROUNDS - 1)
    fir_wait(fir_send)
    for unit in range(UNITS):
        bytes_wait(send_sem.at[unit], NBLK - 1)
    for step in range(ROUNDS):
        for part in range(3):
            copy_twin(step, part).wait_send()
        for lag in range(2):
            copy_across(step, lag).wait_send()


def prepare_kernel(part_ref, small_ref, rec_ref, stage_ref, fir_ref, mate_ref, tt_ref):
    for to in range(NBLK):
        stage_ref[0, to] = rec_ref[:, to * BLOCK : (to + 1) * BLOCK]
        for step in range(ROUNDS):
            which = part_ref[BANKS + step, to].astype(jnp.int32)
            start = pl.multiple_of(which * BLOCK, BLOCK)
            stage_ref[step + 1, to] = rec_ref[:, pl.ds(start, BLOCK)]

    chosen = small_ref[BANKS + ROUNDS : BANKS + ROUNDS + 1, :].astype(jnp.int32)
    fir_ref[...] = jnp.broadcast_to(chosen, (8, BLOCK))
    me = lax.axis_index("chan")
    for step in range(ROUNDS):
        mate_ref[step] = jnp.full((8, BLOCK), part_ref[BANKS + step, me], jnp.float32).astype(jnp.int32)
    tap = lax.broadcasted_iota(jnp.int32, (TAPS, 256), 0)
    lane = lax.broadcasted_iota(jnp.int32, (TAPS, 256), 1)
    flip = (tap + lane == TAPS).astype(jnp.float32)
    turned = jnp.dot(
        small_ref[0:BANKS, 0:TAPS], flip, precision=lax.Precision.HIGHEST, preferred_element_type=jnp.float32
    )
    for b in range(BANKS):
        row = jnp.broadcast_to(turned[b : b + 1, :], (TAPS, 256))
        t = pltpu.roll(row, 0, 1, stride=1, stride_axis=0)[:, : 2 * TAPS]
        high = t.astype(jnp.bfloat16)
        low = (t - high.astype(jnp.float32)).astype(jnp.bfloat16)
        tt_ref[b * TAPS : (b + 1) * TAPS, :] = jnp.concatenate([high, low], axis=1)


def prepare(records, fir_choice, bank, partner):
    smem = pl.BlockSpec(memory_space=pltpu.SMEM)
    vmem = pl.BlockSpec(memory_space=pltpu.VMEM)
    below = 8 - ROUNDS - 1
    whole = jnp.pad(partner, ((BANKS, 8 - ROUNDS), (0, BLOCK - NBLK)))
    whole = whole + jnp.pad(fir_choice[None, :], ((BANKS + ROUNDS, below), (0, 0)))
    small = jnp.pad(bank, ((0, 8), (0, BLOCK - TAPS))) + whole.astype(jnp.float32)
    return pl.pallas_call(
        prepare_kernel,
        in_specs=[smem, vmem, vmem],
        out_specs=[vmem] * 4,
        out_shape=[
            jax.ShapeDtypeStruct((UNITS, NBLK, SPAN, BLOCK), jnp.bfloat16),
            jax.ShapeDtypeStruct((8, BLOCK), jnp.int32),
            jax.ShapeDtypeStruct((ROUNDS, 8, BLOCK), jnp.int32),
            jax.ShapeDtypeStruct((BANKS * TAPS, 256), jnp.bfloat16),
        ],
        compiler_params=pltpu.CompilerParams(vmem_limit_bytes=14 << 20),
        name="prepare",
    )(small, small, records)


def per_device(records, fir_choice, bank, partner):
    ready = prepare(records[0], fir_choice, bank, partner)
    vmem = pl.BlockSpec(memory_space=pltpu.VMEM)
    bf16, f32 = jnp.bfloat16, jnp.float32
    dma = pltpu.SemaphoreType.DMA
    out = pl.pallas_call(
        kernel,
        out_shape=jax.ShapeDtypeStruct((ROUNDS, 2 * BLOCK, BLOCK), f32),
        in_specs=[pl.BlockSpec(memory_space=pl.ANY), vmem, vmem, vmem],
        out_specs=vmem,
        scratch_shapes=[
            pltpu.VMEM((UNITS, TAPS + TIME, BLOCK), bf16),
            pltpu.VMEM((NBLK, 8, BLOCK), jnp.int32),
            pltpu.VMEM((8 + TIME, BLOCK), f32),
            pltpu.VMEM((LAGS * BLOCK, TIME), bf16),
            pltpu.VMEM((TIME, BLOCK), bf16),
            pltpu.VMEM((2 * BLOCK, BLOCK), f32),
            pltpu.VMEM((ROUNDS, 2, 2 * BLOCK, BLOCK), bf16),
            pltpu.VMEM((ROUNDS, 2, 2 * BLOCK, BLOCK), bf16),
            pltpu.VMEM((ROUNDS, 2 * BLOCK, BLOCK), bf16),
            pltpu.VMEM((ROUNDS, 2 * BLOCK, BLOCK), bf16),
            dma((UNITS,)), dma((UNITS, len(GROUPS))), dma((UNITS,)), dma, dma,
            dma((ROUNDS, 3)), dma((ROUNDS, 3)), dma((ROUNDS, 2)), dma((ROUNDS, 2)),
        ],
        compiler_params=pltpu.CompilerParams(
            collective_id=0, has_side_effects=True, vmem_limit_bytes=40 << 20
        ),
        name="correlate",
    )(*ready)
    return out.reshape(ROUNDS, 2, BLOCK, BLOCK).transpose(0, 2, 1, 3)


def solution(mesh):
    placed = (P("rec", "chan", None), P("chan"), P(), P())
    return jax.shard_map(
        per_device,
        mesh=mesh,
        in_specs=placed,
        out_specs=P(None, "chan", "rec", None),
        check_vma=False,
    )
```

```python
import itertools

import jax
import jax.numpy as jnp
from jax import lax
from jax.experimental import pallas as pl
from jax.experimental.pallas import tpu as pltpu
from jax.sharding import PartitionSpec as P

BLOCK = 256
TAPS = 64
LAGS = 8
BANKS = 16
ROUNDS = 3
TIME = 4096
NBLK = 32
SPAN = TIME // NBLK
UNITS = ROUNDS + 1
MESH = pl.DeviceIdType.MESH


def row_pairs():
    groups = []
    for j in range(4):
        dz, dy = j // 2, j % 2
        group = []
        for first, second in ((1, 3), (3, 1), (2, 2), (0, 0)):
            group.append((1 - dz, dy + 2, first))
            group.append((dz, dy, second))
        groups.append(group)
    return groups


GROUPS = row_pairs()
MOVES = [(j, move) for j, group in enumerate(GROUPS) for move in group if move != (0, 0, 0)]


def whiten(raw_ref, tt_ref, choice, ready, last, store):
    def window(w, acc, weight=None):
        base = pl.multiple_of(w * TAPS, TAPS)
        x = raw_ref[pl.ds(base, 2 * TAPS), :]
        every = jnp.dot(
            tt_ref[...], jnp.concatenate([x, x], axis=0), preferred_element_type=jnp.float32
        )
        out = every[0:TAPS]
        for b in range(1, BANKS):
            out = jnp.where(choice == b, every[b * TAPS : (b + 1) * TAPS], out)
        rounded = out.astype(jnp.bfloat16)
        values = rounded.astype(jnp.float32)
        store(base, rounded, values)
        square = (values * values).reshape(TAPS // 8, 8, BLOCK).sum(0)
        return acc + (square if weight is None else square * weight)

    def group(j, acc):
        rows, whole = ready(j)
        for row in rows:
            for inner in range(1, 8):
                acc = window(row * 8 + inner, acc)
        for row in whole:
            missing = (j == 0) | (row == 4)
            skip = jnp.where(missing, 1, 0)
            acc = window(row * 8 + skip, acc, jnp.where(missing, 0.0, 1.0))
        return acc

    acc = lax.fori_loop(0, len(GROUPS), group, jnp.zeros((8, BLOCK), jnp.float32))
    first, second = last
    acc = window(second * 8, window(first * 8, acc))
    acc = window(32, acc, jnp.where((first == 4) | (second == 4), 0.0, 1.0))
    return lax.rsqrt(acc.sum(0, keepdims=True) * (1.0 / TIME) + 1e-6)


def kernel(
    stage, fir_ref, mate_ref, tt_ref, out_ref,
    raw, choices, ownf, shifted, mate, keep, snd1, rcv1, snd2, rcv2,
    send_sem, recv_sem, local_sem, fir_send, fir_recv, s1_send, s1_recv, s2_send, s2_recv,
):
    me = lax.axis_index("chan")
    rec = lax.axis_index("rec")
    mz, my, mx = me // 16, (me // 4) % 4, me % 4
    core, zlo = rec % 2, rec // 2
    twin = zlo * 2 + (1 - core)
    across = (1 - zlo) * 2 + core

    turn = 1 - 2 * core

    def peer(move):
        dz, dy, dx = move
        return ((mz + dz) % 2) * 16 + ((my + 4 + turn * dy) % 4) * 4 + (mx + 4 + turn * dx) % 4

    barrier = pltpu.get_barrier_semaphore()
    for _, move in MOVES:
        pl.semaphore_signal(barrier, inc=1, device_id=(peer(move), rec), device_id_type=MESH)
    pl.semaphore_signal(barrier, inc=1, device_id=(me, twin), device_id_type=MESH)
    pl.semaphore_signal(barrier, inc=1, device_id=(me, across), device_id_type=MESH)
    pl.semaphore_wait(barrier, len(MOVES) + 2)

    mine = pl.ds(pl.multiple_of(TAPS + me * SPAN, TAPS), SPAN)

    def local_copy(unit):
        return pltpu.make_async_copy(stage.at[unit, me], raw.at[unit, mine], local_sem.at[unit])

    def send_unit(unit, carry):
        for j, move in MOVES:
            to = peer(move)
            pltpu.make_async_remote_copy(
                src_ref=stage.at[unit, to],
                dst_ref=raw.at[unit, mine],
                send_sem=send_sem.at[unit],
                recv_sem=recv_sem.at[unit, j],
                device_id=(to, rec),
                device_id_type=MESH,
            ).start()
        local_copy(unit).start()
        raw[unit, 0:TAPS] = jnp.zeros((TAPS, BLOCK), jnp.bfloat16)
        return carry

    send_unit(0, 0)
    for _, move in MOVES:
        pltpu.make_async_remote_copy(
            src_ref=fir_ref,
            dst_ref=choices.at[me],
            send_sem=fir_send,
            recv_sem=fir_recv,
            device_id=(peer(move), rec),
            device_id_type=MESH,
        ).start()
    choices[me] = fir_ref[...]
    lax.fori_loop(1, UNITS - 1, send_unit, 0)

    def bytes_wait(sem, pieces):
        view = raw.at[0, pl.ds(0, pieces * SPAN)]
        pltpu.make_async_copy(view, view, sem).wait()

    def rows_of(j):
        dz, dy = j // 2, j % 2
        first = ((mz + dz) % 2) * 4 + (my + 4 - turn * dy) % 4
        second = ((mz + 1 - dz) % 2) * 4 + (my + 8 - turn * (dy + 2)) % 4
        return first, second

    last = rows_of((1 - core) * 3)

    def arrival(unit):
        def ready(j):
            @pl.when(j == 0)
            def _():
                bytes_wait(recv_sem.at[unit, j], 7)
                local_copy(unit).wait()

            @pl.when(j > 0)
            def _():
                bytes_wait(recv_sem.at[unit, j], 8)

            before = jnp.where(core == 0, jnp.maximum(j - 1, 0), j)
            return rows_of(j), rows_of(before)

        return ready

    def fir_wait(sem):
        view = choices.at[pl.ds(0, NBLK - 1)]
        pltpu.make_async_copy(view, view, sem).wait()

    ownf[0:8] = jnp.zeros((8, BLOCK), jnp.float32)

    def store_own(base, rounded, values):
        ownf[pl.ds(base + 8, TAPS)] = values

    inv_own = whiten(raw.at[0], tt_ref, fir_ref[0:1], arrival(0), last, store_own)
    send_unit(UNITS - 1, 0)

    def shift(d, carry):
        base = pl.multiple_of(d * 128, 128)
        y = ownf[pl.ds(base, 136)] * inv_own
        for lag in range(LAGS):
            row = ((lag // 2) % 2) * 4 + (lag // 4) * 2 + lag % 2
            shifted[row * BLOCK : (row + 1) * BLOCK, pl.ds(base, 128)] = (
                y[8 - lag : 136 - lag].astype(jnp.bfloat16).T
            )
        return carry

    lax.fori_loop(0, TIME // 128, shift, 0, unroll=2)
    fir_wait(fir_recv)

    def store_mate(base, rounded, values):
        mate[pl.ds(base, TAPS)] = rounded

    def product(to_core, to_zlo, first, count):
        start = ((to_core * 2 + to_zlo) * 2 + first) * BLOCK
        rows = pl.ds(pl.multiple_of(start, BLOCK), count * BLOCK)
        return jnp.dot(shifted[rows], mate[...], preferred_element_type=jnp.float32)

    def copy_twin(step, part):
        if part == 2:
            where = (step, 1)
        else:
            where = (step, 0, pl.ds(part * BLOCK, BLOCK))
        return pltpu.make_async_remote_copy(
            src_ref=snd1.at[where],
            dst_ref=rcv1.at[where],
            send_sem=s1_send.at[step, part],
            recv_sem=s1_recv.at[step, part],
            device_id=(me, twin),
            device_id_type=MESH,
        )

    def copy_across(step, lag):
        where = (step, pl.ds(lag * BLOCK, BLOCK))
        return pltpu.make_async_remote_copy(
            src_ref=snd2.at[where],
            dst_ref=rcv2.at[where],
            send_sem=s2_send.at[step, lag],
            recv_sem=s2_recv.at[step, lag],
            device_id=(me, across),
            device_id_type=MESH,
        )

    def finish(step):
        for lag in range(2):
            here = slice(lag * BLOCK, (lag + 1) * BLOCK)
            copy_across(step, lag).wait_recv()
            out_ref[step, here] = out_ref[step, here] + rcv2[step, here].astype(jnp.float32)

    def round_body(step, carry):
        which = mate_ref[step]
        choice = choices[0]
        for block in range(1, NBLK):
            choice = jnp.where(which == block, choices[block], choice)
        choice = choice[0:1]
        inv = whiten(raw.at[step + 1], tt_ref, choice, arrival(step + 1), last, store_mate)
        scale = inv * (TIME**-0.5)
        for lag in range(2):
            here = slice(lag * BLOCK, (lag + 1) * BLOCK)
            away = product(1 - core, 1 - zlo, lag, 1) * scale
            snd1[step, 0, here] = away.astype(jnp.bfloat16)
            copy_twin(step, lag).start()
        for lag in range(2):
            here = slice(lag * BLOCK, (lag + 1) * BLOCK)
            keep[here] = product(core, 1 - zlo, lag, 1) * scale
            copy_twin(step, lag).wait_recv()
            both = keep[here] + rcv1[step, 0, here].astype(jnp.float32)
            snd2[step, here] = both.astype(jnp.bfloat16)
            copy_across(step, lag).start()
        snd1[step, 1] = (product(1 - core, zlo, 0, 2) * scale).astype(jnp.bfloat16)
        copy_twin(step, 2).start()
        keep[...] = product(core, zlo, 0, 2) * scale
        copy_twin(step, 2).wait_recv()
        out_ref[step] = keep[...] + rcv1[step, 1].astype(jnp.float32)

        @pl.when(step > 0)
        def _():
            finish(step - 1)

        return carry

    lax.fori_loop(0, ROUNDS, round_body, 0)
    finish(ROUNDS - 1)
    fir_wait(fir_send)
    for unit in range(UNITS):
        bytes_wait(send_sem.at[unit], NBLK - 1)
    for step in range(ROUNDS):
        for part in range(3):
            copy_twin(step, part).wait_send()
        for lag in range(2):
            copy_across(step, lag).wait_send()


def prepare_kernel(part_ref, small_ref, rec_ref, stage_ref, fir_ref, mate_ref, tt_ref):
    for to in range(NBLK):
        stage_ref[0, to] = rec_ref[:, to * BLOCK : (to + 1) * BLOCK]
        for step in range(ROUNDS):
            which = part_ref[BANKS + step, to].astype(jnp.int32)
            start = pl.multiple_of(which * BLOCK, BLOCK)
            stage_ref[step + 1, to] = rec_ref[:, pl.ds(start, BLOCK)]

    chosen = small_ref[BANKS + ROUNDS : BANKS + ROUNDS + 1, :].astype(jnp.int32)
    fir_ref[...] = jnp.broadcast_to(chosen, (8, BLOCK))
    me = lax.axis_index("chan")
    for step in range(ROUNDS):
        mate_ref[step] = jnp.full((8, BLOCK), part_ref[BANKS + step, me], jnp.float32).astype(jnp.int32)
    tap = lax.broadcasted_iota(jnp.int32, (TAPS, 256), 0)
    lane = lax.broadcasted_iota(jnp.int32, (TAPS, 256), 1)
    flip = (tap + lane == TAPS).astype(jnp.float32)
    turned = jnp.dot(
        small_ref[0:BANKS, 0:TAPS], flip, precision=lax.Precision.HIGHEST, preferred_element_type=jnp.float32
    )
    for b in range(BANKS):
        row = jnp.broadcast_to(turned[b : b + 1, :], (TAPS, 256))
        t = pltpu.roll(row, 0, 1, stride=1, stride_axis=0)[:, : 2 * TAPS]
        high = t.astype(jnp.bfloat16)
        low = (t - high.astype(jnp.float32)).astype(jnp.bfloat16)
        tt_ref[b * TAPS : (b + 1) * TAPS, :] = jnp.concatenate([high, low], axis=1)


def prepare(records, fir_choice, bank, partner):
    smem = pl.BlockSpec(memory_space=pltpu.SMEM)
    vmem = pl.BlockSpec(memory_space=pltpu.VMEM)
    below = 8 - ROUNDS - 1
    whole = jnp.pad(partner, ((BANKS, 8 - ROUNDS), (0, BLOCK - NBLK)))
    whole = whole + jnp.pad(fir_choice[None, :], ((BANKS + ROUNDS, below), (0, 0)))
    small = jnp.pad(bank, ((0, 8), (0, BLOCK - TAPS))) + whole.astype(jnp.float32)
    return pl.pallas_call(
        prepare_kernel,
        in_specs=[smem, vmem, vmem],
        out_specs=[vmem] * 4,
        out_shape=[
            jax.ShapeDtypeStruct((UNITS, NBLK, SPAN, BLOCK), jnp.bfloat16),
            jax.ShapeDtypeStruct((8, BLOCK), jnp.int32),
            jax.ShapeDtypeStruct((ROUNDS, 8, BLOCK), jnp.int32),
            jax.ShapeDtypeStruct((BANKS * TAPS, 256), jnp.bfloat16),
        ],
        compiler_params=pltpu.CompilerParams(vmem_limit_bytes=14 << 20),
        name="prepare",
    )(small, small, records)


def per_device(records, fir_choice, bank, partner):
    ready = prepare(records[0], fir_choice, bank, partner)
    vmem = pl.BlockSpec(memory_space=pltpu.VMEM)
    bf16, f32 = jnp.bfloat16, jnp.float32
    dma = pltpu.SemaphoreType.DMA
    out = pl.pallas_call(
        kernel,
        out_shape=jax.ShapeDtypeStruct((ROUNDS, 2 * BLOCK, BLOCK), f32),
        in_specs=[pl.BlockSpec(memory_space=pl.ANY), vmem, vmem, vmem],
        out_specs=vmem,
        scratch_shapes=[
            pltpu.VMEM((UNITS, TAPS + TIME, BLOCK), bf16),
            pltpu.VMEM((NBLK, 8, BLOCK), jnp.int32),
            pltpu.VMEM((8 + TIME, BLOCK), f32),
            pltpu.VMEM((LAGS * BLOCK, TIME), bf16),
            pltpu.VMEM((TIME, BLOCK), bf16),
            pltpu.VMEM((2 * BLOCK, BLOCK), f32),
            pltpu.VMEM((ROUNDS, 2, 2 * BLOCK, BLOCK), bf16),
            pltpu.VMEM((ROUNDS, 2, 2 * BLOCK, BLOCK), bf16),
            pltpu.VMEM((ROUNDS, 2 * BLOCK, BLOCK), bf16),
            pltpu.VMEM((ROUNDS, 2 * BLOCK, BLOCK), bf16),
            dma((UNITS,)), dma((UNITS, len(GROUPS))), dma((UNITS,)), dma, dma,
            dma((ROUNDS, 3)), dma((ROUNDS, 3)), dma((ROUNDS, 2)), dma((ROUNDS, 2)),
        ],
        compiler_params=pltpu.CompilerParams(
            collective_id=0, has_side_effects=True, vmem_limit_bytes=40 << 20
        ),
        name="correlate",
    )(*ready)
    return out.reshape(ROUNDS, 2, BLOCK, BLOCK).transpose(0, 2, 1, 3)


def solution(mesh):
    placed = (P("rec", "chan", None), P("chan"), P(), P())
    return jax.shard_map(
        per_device,
        mesh=mesh,
        in_specs=placed,
        out_specs=P(None, "chan", "rec", None),
        check_vma=False,
    )
```
